256 devices in a mesh: grp: 8 (over y, core), dev: 32 (over x, z).
Axes of the slice: x: 4, y: 4, z: 8, core: 2. Of those that a mesh axis runs over, the one named last changes fastest.
Arguments:
- table: bfloat16 [65536, 256], P('dev'), may hold values from -4 to 4
- hist_bias: float32 [524288], P(('grp', 'dev')), may hold values from -3 to 303
- hist_shard: int32 [524288, 1], P(('grp', 'dev')), may hold values from 0 to 31; in each aligned block of 2048 rows (0 to 2047, 2048 to 4095, ...) at most 96 rows name the same one
- hist_row: int32 [524288], P(('grp', 'dev')), may hold values from 0 to 2047
- lengths: int32 [256, 4], P(('grp', 'dev')), may hold values from 1 to 1024, 2048 in all within a row
- panel_row: int32 [8192], P(('grp', 'dev')), may hold values from 0 to 2047
- req_user: int32 [524288], P(('grp', 'dev')), may hold values from 0 to 3
- req_cand: int32 [524288], P(('grp', 'dev')), may hold values from 0 to 1023
- d_out: bfloat16 [524288, 256], P(('grp', 'dev')), may hold values from -6 to 6
Outputs:
- attended: bfloat16 [524288, 256], P(('grp', 'dev'))
- table_grad: float32 [32, 2048, 256], P('dev', 'grp')
- bias_grad: float32 [524288], P(('grp', 'dev'))
The draws below stay inside these ranges and needn't reach their ends.
Inputs may be any that keep to these rules, and one draw needn't show every extreme that they name: `hist_shard`: among the 2048 history entries of one device at most 96 name the same shard, and some device's entries name some shard exactly 96 times. `lengths`: each row sums to 2048, and its largest entry is exactly 1024.
All inputs are finite; a program needn't handle non-finite values.
Results may differ from the reference program's by a relative error of at most 0.018.
Values may be sent and summed in bfloat16 or wider, within the bound.
No kernel may reach another device: no remote copies, remote signals or barrier semaphores. Data moves between devices by JAX's collectives and lax.ppermute only.
A program may use at most 64 MiB of HBM per device.

```python
import math
import jax
import jax.numpy as jnp
import numpy as np
from jax import lax

D = 256
L = 1024
U_DEV = 4
R_DEV = 2048
V_DEV = 2048
CP_DEV = 32
H_DEV = 2048
CAP = 96
P_GRP = 1024
HIST = 524288
REQS = 524288
PANEL = 8192
TROWS = 65536
N_GRP = 8
N_DEV = 32
DEVICES = 256


def draw_hist_bias(key, part):
    key = jax.random.fold_in(key, 7)
    return jax.random.uniform(key, (HIST,), jnp.float32, -3.0, 3.0)


def plant(values, rng, least, top_value):
    longest = values.shape.index(max(values.shape))
    spots = []
    for shift in (0, 1):
        where = [jax.random.randint(jax.random.fold_in(rng, axis), (), 0, length) for axis, length in enumerate(values.shape)]
        where[longest] = (where[longest] + shift) % values.shape[longest]
        spots.append(tuple(where))
    return values.at[spots[0]].set(least).at[spots[1]].set(top_value)


def shard_levels(stream_key, dims, cuts, least, largest):
    def one(axis_at, parts):
        heights = jax.random.uniform(jax.random.fold_in(jax.random.fold_in(stream_key, 6), axis_at), (parts,), jnp.float32, least / len(cuts), largest / len(cuts))
        return jnp.repeat(jnp.exp(heights), dims[axis_at] // parts).reshape((-1,) + (1,) * (len(dims) - axis_at - 1))

    gain = one(*cuts[0])
    for cut in cuts[1:]:
        gain = gain * one(*cut)
    return gain


def length_profile(amount, total, limit, lean):
    portions = [(1 << 20) // math.isqrt(rank ** lean) + 1 for rank in range(2, amount + 1)]
    rest, counts = total - limit - (amount - 1), [1] * (amount - 1)
    while rest > 0:
        movable = [i for i in range(amount - 1) if counts[i] < limit]
        pool, budget = sum([portions[i] for i in movable]), rest
        for i in movable:
            extra = min(limit - counts[i], max(1, budget * portions[i] // pool), rest)
            counts[i] = counts[i] + extra
            rest = rest - extra
    return np.array([limit] + counts)


def uneven(stream_key, amount, total, reach, slope):
    if amount == 2:
        one = jax.random.randint(stream_key, (), max(1, total - reach), min(reach, total - 1) + 1)
        return jnp.stack([one, total - one])
    sizes = jnp.asarray(length_profile(amount, total, reach, slope), jnp.int32)
    twos = (amount - 1) // 2
    source_of, receiver = sizes[1:1 + 2 * twos:2], sizes[2:2 + 2 * twos:2]
    margin = jnp.minimum(source_of - 1, reach - receiver)
    shifted = jax.random.randint(jax.random.fold_in(stream_key, 1), (twos,), 0, 1 << 20) % (margin + 1)
    sizes = sizes.at[1:1 + 2 * twos:2].set(source_of - shifted).at[2:2 + 2 * twos:2].set(receiver + shifted)
    return sizes[jax.random.permutation(jax.random.fold_in(stream_key, 2), amount)]


def shared_out(stream_key, own, number, rows, amount, top, bound, slope):
    order = jax.random.permutation(stream_key, amount)
    heavy_load, ordinary = portions_of(amount, rows * top, bound, slope, True), portions_of(amount, rows * top, bound, slope, False)
    places = jnp.arange(amount)

    def named(tallies, rotation):
        used = int((tallies > 0).sum())
        fixed = max(1, used // 4)
        shifted = fixed + (places - fixed + rotation * (used - fixed)) % max(1, amount - fixed)
        return jnp.zeros((amount,), jnp.int32).at[order[jnp.where(places < fixed, places, shifted)]].set(jnp.asarray(tallies, jnp.int32))

    tallies = jnp.where(number % 4 == 0, named(heavy_load, number // 4), named(ordinary, number - number // 4 - 1))
    mixed = jax.random.permutation(jax.random.fold_in(own, 3), amount)
    donor, sink = mixed[0:amount // 2 * 2:2], mixed[1:amount // 2 * 2:2]
    margin = jnp.minimum(tallies[donor] - 1, bound - tallies[sink]) // 2
    margin = jnp.where((donor == order[0]) | (sink == order[0]) | (tallies[sink] == 0), 0, jnp.maximum(margin, 0))
    shifted = jax.random.randint(jax.random.fold_in(own, 4), (amount // 2,), 0, 1 << 20) % (margin + 1)
    tallies = tallies.at[donor].add(-shifted).at[sink].add(shifted)
    members = jnp.searchsorted(jnp.cumsum(tallies), jnp.arange(rows * top), side="right").astype(jnp.int32)
    listing = members.reshape(top, rows).T
    listing = listing[jax.random.permutation(jax.random.fold_in(own, 1), rows)]
    rotation = jax.random.randint(jax.random.fold_in(own, 2), (rows, 1), 0, top)
    return jnp.take_along_axis(listing, (jnp.arange(top)[None, :] + rotation) % top, axis=1)


def portions_of(number_of, total, limit, slope, full):
    weights = [(1 << 20) // math.isqrt(rank ** slope) + 1 for rank in range(1, number_of + 1)]
    largest = limit if full else min(limit, max(-(-total // number_of), total * weights[0] // sum(weights)))
    least = 1 if total - largest >= number_of - 1 else 0
    given, rest = [largest] + [least] * (number_of - 1), total - largest - least * (number_of - 1)
    while rest > 0:
        candidates = [i for i in range(1, number_of) if given[i] < largest] or [i for i in range(1, number_of) if given[i] < limit]
        mass, left = sum([weights[i] for i in candidates]), rest
        for i in candidates:
            addition = min(limit - given[i], max(1, left * weights[i] // mass), rest)
            given[i] = given[i] + addition
            rest = rest - addition
    return np.array(given)


def bell_draw(rng, dims, scale, limit, shards=(), held_as=jnp.bfloat16):
    entries = jax.random.normal(rng, dims, jnp.float32) * scale
    if len(shards) > 0:
        entries = shard_levels(rng, dims, shards, -0.22, 0.18) * entries
    return jnp.clip(entries, min=-limit, max=limit).astype(held_as)


def setup_inputs(seed: int = 0) -> dict:
    key_of = jax.random.split(jax.random.key(seed), 10)
    table = bell_draw(key_of[0], (TROWS, D), 1.0, 4.0, ((0, 32),))
    hist_bias = draw_hist_bias(jax.random.fold_in(key_of[9], 71), 0)
    hist_shard_keys = jax.random.split(jax.random.fold_in(key_of[2], 1), HIST // H_DEV)
    hist_shard_turns = jax.random.permutation(jax.random.fold_in(key_of[2], 3), HIST // H_DEV)
    hist_shard = jax.vmap(lambda own, number: shared_out(jax.random.fold_in(key_of[2], 2), own, number, H_DEV, N_DEV, 1, CAP, 1))(hist_shard_keys, hist_shard_turns).reshape((HIST, 1))
    hist_row = plant(jax.random.randint(key_of[3], (HIST,), 0, V_DEV), jax.random.fold_in(key_of[3], 1), 0, V_DEV - 1).astype(jnp.int32)
    lengths = jax.vmap(lambda own: uneven(own, U_DEV, H_DEV, L, 1))(jax.random.split(key_of[4], DEVICES)).reshape((DEVICES, U_DEV)).astype(jnp.int32)
    panel_row = plant(jax.random.randint(key_of[5], (PANEL,), 0, V_DEV), jax.random.fold_in(key_of[5], 1), 0, V_DEV - 1).astype(jnp.int32)
    req_user = plant(jax.random.randint(key_of[6], (REQS,), 0, U_DEV), jax.random.fold_in(key_of[6], 1), 0, U_DEV - 1).astype(jnp.int32)
    req_cand = plant(jax.random.randint(key_of[7], (REQS,), 0, P_GRP), jax.random.fold_in(key_of[7], 1), 0, P_GRP - 1).astype(jnp.int32)
    d_out = bell_draw(key_of[8], (REQS, D), 1.0, 6.0, ((0, 256),))
    return dict(table=table, hist_bias=hist_bias, hist_shard=hist_shard, hist_row=hist_row, lengths=lengths, panel_row=panel_row, req_user=req_user, req_cand=req_cand, d_out=d_out)


def attend_block(queries, key_rows, key_bias, segment, owners, grad_out):
    scaling = queries.shape[-1] ** (-0.5)
    scores = lax.dot_general(queries, key_rows, (((1,), (1,)), ((), ())), preferred_element_type=jnp.float32)
    scores = scores * scaling + key_bias[None, :]
    allowed = owners[:, None] == segment[None, :]
    masked = jnp.where(allowed, scores, -1e+30)
    row_top = lax.optimization_barrier(jnp.max(masked, axis=1, keepdims=True))
    raised = jnp.where(allowed, jnp.exp(masked - row_top), 0.0)
    totals = lax.optimization_barrier(jnp.sum(raised, axis=1, keepdims=True))
    weights = raised / totals
    weights_b = weights.astype(jnp.bfloat16)
    mixed = jnp.dot(weights_b, key_rows, preferred_element_type=jnp.float32)
    power = lax.optimization_barrier(jnp.mean(mixed * mixed, axis=1, keepdims=True))
    inverse = lax.rsqrt(power + 1e-06)
    attended = (mixed * inverse).astype(jnp.bfloat16)
    upstream = grad_out.astype(jnp.float32)
    along = lax.optimization_barrier(jnp.mean(upstream * mixed, axis=1, keepdims=True))
    d_mixed_b = (inverse * upstream - mixed * inverse * inverse * inverse * along).astype(jnp.bfloat16)
    d_weights = lax.dot_general(d_mixed_b, key_rows, (((1,), (1,)), ((), ())), preferred_element_type=jnp.float32)
    d_scores = weights * (d_weights - lax.optimization_barrier(jnp.sum(weights * d_weights, axis=1, keepdims=True)))
    d_bias = lax.optimization_barrier(jnp.sum(d_scores, axis=0))
    d_scores_b = (d_scores * scaling).astype(jnp.bfloat16)
    d_queries = jnp.dot(d_scores_b, key_rows, preferred_element_type=jnp.float32)
    d_keys = lax.dot_general(weights_b, d_mixed_b, (((0,), (0,)), ((), ())), preferred_element_type=jnp.float32)
    d_keys = d_keys + lax.dot_general(d_scores_b, queries, (((0,), (0,)), ((), ())), preferred_element_type=jnp.float32)
    return (attended, d_queries, d_keys, d_bias)

def attend_all(queries, key_rows, key_bias, segment, owners, grad_out):
    rows_all = queries.shape[0]
    block_rows = min(512, rows_all)
    blocks = rows_all // block_rows
    width = queries.shape[1]
    start = (jnp.zeros(key_rows.shape, jnp.float32), jnp.zeros(key_bias.shape, jnp.float32))

    def advance(carry, piece):
        attended, d_queries, d_keys, d_bias = attend_block(piece[0], key_rows, key_bias, segment, piece[1], piece[2])
        return ((carry[0] + d_keys, carry[1] + d_bias), (attended, d_queries))
    pieces = (queries.reshape(blocks, block_rows, width), owners.reshape(blocks, block_rows), grad_out.reshape(blocks, block_rows, width))
    (d_keys, d_bias), (attended, d_queries) = lax.scan(advance, start, pieces)
    return (attended.reshape(rows_all, width), d_queries.reshape(rows_all, width), d_keys, d_bias)

def segments_of(length_row, hist_len):
    seg_ends = jnp.cumsum(length_row)
    places = jnp.arange(hist_len, dtype=jnp.int32)
    return lax.optimization_barrier(jnp.sum((places[:, None] >= seg_ends[None, :]).astype(jnp.int32), axis=1))

def reference(table, hist_bias, hist_shard, hist_row, lengths, panel_row, req_user, req_cand, d_out):
    item_ids = (hist_shard[:, 0] * V_DEV + hist_row).reshape(DEVICES, H_DEV)
    contributor = jnp.arange(PANEL, dtype=jnp.int32) // CP_DEV % N_DEV
    panel_items = (contributor * V_DEV + panel_row).reshape(N_GRP, P_GRP)
    xs = (jnp.arange(DEVICES, dtype=jnp.int32), item_ids, hist_bias.reshape(DEVICES, H_DEV), lengths, req_user.reshape(DEVICES, R_DEV), req_cand.reshape(DEVICES, R_DEV), d_out.reshape(DEVICES, R_DEV, D))

    def advance(grad_all, piece):
        device, own_items, own_bias, own_lengths, own_users, own_cands, own_grad = piece
        group_items = panel_items[device // N_DEV]
        key_rows = table[own_items]
        queries = table[group_items[own_cands]]
        segment = segments_of(own_lengths, H_DEV)
        attended, d_queries, d_keys, d_bias = attend_all(queries, key_rows, own_bias, segment, own_users, own_grad)
        panel_terms = jax.ops.segment_sum(d_queries, own_cands, num_segments=P_GRP).astype(jnp.bfloat16)
        panel_terms = lax.optimization_barrier(panel_terms).astype(jnp.float32)
        key_terms = lax.optimization_barrier(d_keys.astype(jnp.bfloat16)).astype(jnp.float32)
        grad_all = grad_all.at[group_items].add(panel_terms)
        grad_all = grad_all.at[own_items].add(key_terms)
        return (grad_all, (attended, d_bias))
    grad_all, (attended, bias_grad) = lax.scan(advance, jnp.zeros((TROWS, D), jnp.float32), xs)
    return (attended.reshape(REQS, D), grad_all.reshape(N_DEV, V_DEV, D), bias_grad.reshape(HIST))
```

```python
import functools

import jax
import jax.numpy as jnp
from jax import lax
from jax.experimental import pallas as pl
from jax.experimental.pallas import tpu as pltpu
from jax.sharding import PartitionSpec as P

BF = jnp.bfloat16
F32 = jnp.float32
I32 = jnp.int32
H = 2048
D = 256
NS = 32
CAP = 96
CP = 32
ASK = 40
PG = NS * CP
TILE = 256
WIDTHS = (256, 512, 768, 1024, 1280, 1536, 2048)
MB = 1 << 20

VM = pl.BlockSpec(memory_space=pltpu.VMEM)
SM = pl.BlockSpec(memory_space=pltpu.SMEM)
HB = pl.BlockSpec(memory_space=pltpu.HBM)


def iota(shape, dim):
    return lax.broadcasted_iota(I32, shape, dim)


def mm(a, b):
    return jnp.dot(a, b, preferred_element_type=F32)


def mm_nt(a, b):
    return lax.dot_general(a, b, (((1,), (1,)), ((), ())), preferred_element_type=F32)


def ones_where(mask):
    return jnp.where(mask, 1.0, 0.0).astype(BF)


def onehot_lanes(column, count):
    lane = iota(column.shape, 1).astype(column.dtype)
    return jnp.concatenate(
        [ones_where(column == lane + 128 * t) for t in range(count // 128)], axis=1
    )


def onehot_rows(row, base, count):
    return ones_where(iota((count, row.shape[1]), 0) + base == row)


def as_column(row):
    return jnp.transpose(jnp.broadcast_to(row.astype(F32), (128, row.shape[1])))


def ranks(member):
    width = 256
    upper = ones_where(iota((width, width), 0) < iota((width, width), 1))
    ahead, carry = [], jnp.zeros((member.shape[0], 1), F32)
    for b in range(member.shape[1] // width):
        part = member[:, b * width : (b + 1) * width]
        ahead.append(mm(part.astype(BF), upper) + carry)
        carry = carry + jnp.sum(part, axis=1, keepdims=True)
    return jnp.sum(jnp.concatenate(ahead, axis=1) * member, axis=0, keepdims=True)


def prepare_kernel(shard, row, panel_row, table, slot, out):
    target = shard[...]
    member = jnp.where(iota((NS, H), 0) == target, 1.0, 0.0)
    rank = ranks(member).astype(I32)
    slot[...] = target * CAP + rank
    here = iota((128, H), 0) == rank
    low = jnp.where(here, (row[...] & 127).astype(F32), 0.0).astype(BF)
    high = jnp.where(here, (row[...] >> 7).astype(F32), 0.0).astype(BF)
    ids = mm_nt(member.astype(BF), jnp.concatenate([low, high], axis=0))
    own = jnp.zeros((CP, 128), I32)
    for c in range(CP):
        own = jnp.where(iota((CP, 128), 0) == c, panel_row[c], own)
    rows = mm(onehot_lanes(own, H), table[...])
    pad = jnp.zeros((ASK - CP - 1, D), F32)
    for s in range(NS):
        out[s] = jnp.concatenate([rows, ids[s : s + 1, :], pad], axis=0).astype(BF)


def fetch_kernel(first, table, asked, panel, out, rows, sems):
    both = [first[s].astype(F32)[CP : CP + 1, :] for s in range(NS)]
    both = jnp.concatenate(both, axis=0)
    ids = both[:, :128] + 128.0 * both[:, 128:]
    asked[...] = ids.astype(I32)
    ids = jnp.transpose(jnp.concatenate([ids, jnp.zeros((96, 128), F32)], axis=0))
    copies = []
    for n in range(4):
        part = pl.ds(n * 8, 8)
        hot = jnp.concatenate(
            [
                onehot_lanes(jnp.broadcast_to(ids[:CAP, s : s + 1], (CAP, 128)), H)
                for s in range(n * 8, n * 8 + 8)
            ],
            axis=0,
        )
        rows[part] = mm(hot, table[...]).astype(BF).reshape(8, CAP, D)
        copies.append(pltpu.make_async_copy(rows.at[part], out.at[part], sems.at[n]))
        copies[-1].start()
    for s in range(NS):
        panel[s * CP : s * CP + CP, :] = first[s, :CP, :]
    for copy in copies:
        copy.wait()


def requests_kernel(
    user, cand, bias, slot, d_out, panel, q, q_t, up_t, slot_col, bias_col, pos_col, cand_row, starts
):
    own = user[...]
    member = jnp.where(iota((8, H), 0) == own, 1.0, 0.0)
    pos = ranks(member)
    begin = [jnp.sum(jnp.where(own < u, 1.0, 0.0)).astype(I32) for u in (1, 2, 3)]
    starts[0] = 0
    for u in (1, 2, 3):
        starts[u] = begin[u - 1]
        pos = pos + jnp.where(own == u, begin[u - 1].astype(F32), 0.0)
    pos = pos.astype(I32)
    slot_col[...] = as_column(slot[...]).astype(I32)
    bias_col[...] = as_column(bias[...])
    pos_col[...] = as_column(pos).astype(I32)
    low = as_column(cand[...] & 127).astype(BF)
    high = as_column(cand[...] >> 7).astype(BF)
    right = jnp.concatenate([d_out[...], low, high], axis=1)
    for i in range(4):
        part = slice(i * 512, (i + 1) * 512)
        got = mm(onehot_rows(pos, i * 512, 512), right)
        up_t[:, part] = jnp.transpose(got[:, :D]).astype(BF)
        which = got[:, D : D + 128] + 128.0 * got[:, D + 128 :]
        cand_row[:, part] = jnp.transpose(which)[:1, :].astype(I32)
        query = mm(onehot_lanes(which, PG), panel[...]) * (D**-0.5)
        q[part, :] = query.astype(BF)
        q_t[:, part] = jnp.transpose(query).astype(BF)


def attend_kernel(
    got, slot, cand_row, lengths, starts, slot_hbm, bias_hbm, q_hbm, q_t_hbm, up_t_hbm,
    bias_grad, att_hbm, send_hbm,
    slot_col, bias_col, q, q_t, up_t, att_t, send,
    key, key_t, seg, d_key, d_bias, dq_t, sems,
):
    loads = [
        pltpu.make_async_copy(a, b, sems.at[n])
        for n, (a, b) in enumerate(
            [
                (slot_hbm, slot_col),
                (bias_hbm, bias_col),
                (q_t_hbm, q_t),
                (up_t_hbm, up_t),
                (q_hbm, q),
            ]
        )
    ]
    for load in loads:
        load.start()
    loads[0].wait()
    for i in range(4):
        part = slice(i * 512, (i + 1) * 512)
        rows = mm(onehot_lanes(slot_col[part, :], NS * CAP), got[...])
        key[part, :] = rows.astype(BF)
        key_t[:, part] = jnp.transpose(rows).astype(BF)
    ends = [lengths[0]]
    for u in (1, 2, 3):
        ends.append(ends[-1] + lengths[u])
    place = iota((H, 128), 0)
    seg[...] = sum((place >= ends[u]).astype(I32) for u in range(3))
    d_key[...] = jnp.zeros_like(d_key)
    d_bias[...] = jnp.zeros_like(d_bias)

    for load in loads[1:]:
        load.wait()

    def owner_of(r):
        return sum((r >= starts[u]).astype(I32) for u in (1, 2, 3))

    def step(i, width, first):
        cols = pl.ds(pl.multiple_of(i * TILE, TILE), TILE)
        first = pl.multiple_of(first, 128)
        win = pl.ds(first, width)
        r = iota((1, TILE), 1) + i * TILE
        owner = owner_of(r)
        k = key[win, :]
        bias2 = bias_col[win, :]
        seg2 = seg[win, :]
        score = mm(k, q_t[:, cols]) + jnp.concatenate([bias2, bias2], axis=1)
        score = jnp.where(jnp.concatenate([seg2, seg2], axis=1) == owner, score, -1e30)
        raised = jnp.exp(score - jnp.max(score, axis=0, keepdims=True))
        weight = raised * (1.0 / jnp.sum(raised, axis=0, keepdims=True))
        weight_b = weight.astype(BF)
        mixed = mm(key_t[:, win], weight_b)
        inverse = lax.rsqrt(jnp.mean(mixed * mixed, axis=0, keepdims=True) + 1e-6)
        att_t[:, cols] = (mixed * inverse).astype(BF)
        up = up_t[:, cols].astype(F32)
        along = jnp.mean(up * mixed, axis=0, keepdims=True)
        d_mixed = inverse * up - mixed * (inverse * inverse * inverse * along)
        d_mixed_b = d_mixed.astype(BF)
        rounded = d_mixed_b.astype(F32)
        d_weight = mm(k, d_mixed_b)
        total = jnp.sum(rounded * mixed, axis=0, keepdims=True)
        d_score = weight * (d_weight - total)
        d_bias[win, :] += d_score[:, :128] + d_score[:, 128:]
        d_score_b = d_score.astype(BF)
        left = jnp.concatenate([weight_b, d_score_b], axis=1)
        right = jnp.concatenate([jnp.transpose(rounded).astype(BF), q[cols, :]], axis=0)
        d_key[win, :] += mm(left, right)
        dq_t[:, cols] = (mm(key_t[:, win], d_score_b) * (D**-0.5)).astype(BF)

    def tile(i, carry):
        u_first = owner_of(i * TILE)
        u_last = owner_of(i * TILE + TILE - 1)
        low, high = jnp.int32(0), ends[0]
        for u in (1, 2, 3):
            low = jnp.where(u_first >= u, ends[u - 1], low)
            high = jnp.where(u_last >= u, ends[u], high)
        first = (low // 128) * 128
        need = high - first
        for n, width in enumerate(WIDTHS):
            fits = need <= width
            if n > 0:
                fits = fits & (need > WIDTHS[n - 1])

            @pl.when(fits)
            def _():
                step(i, width, jnp.minimum(first, H - width))

        return carry

    lax.fori_loop(0, H // TILE, tile, 0)
    stores = [pltpu.make_async_copy(att_t, att_hbm, sems.at[5])]
    stores[0].start()
    term = d_key[...].astype(BF)
    for n in range(4):
        part = pl.ds(n * 8, 8)
        out = mm(onehot_rows(slot[...], n * 8 * CAP, 8 * CAP), term).astype(BF)
        send[part, :CAP, :] = out.reshape(8, CAP, D)
        out = mm_nt(onehot_rows(cand_row[...], n * 8 * CP, 8 * CP), dq_t[...]).astype(BF)
        send[part, CAP:, :] = out.reshape(8, CP, D)
        stores.append(
            pltpu.make_async_copy(send.at[part], send_hbm.at[part], sems.at[6 + n])
        )
        stores[-1].start()
    bias_grad[...] = jnp.sum(jnp.transpose(d_bias[...]), axis=0, keepdims=True)
    for store in stores:
        store.wait()


def restore_kernel(pos_col, att_t, out):
    for i in range(4):
        part = slice(i * 512, (i + 1) * 512)
        out[part, :] = mm_nt(onehot_lanes(pos_col[part, :], H), att_t[...]).astype(BF)


def gradient_kernel(place, panel_row, asked, arrived, out):
    ids = asked[...]
    lane = iota((1, 128), 1)
    own = jnp.zeros((1, 128), I32)
    for c in range(CP):
        own = jnp.where(lane == CAP + c, panel_row[c], own)
    ids = jnp.concatenate(
        [jnp.where(lane >= CAP, own, ids[s : s + 1, :]) for s in range(NS)], axis=1
    )
    rows = arrived[...].reshape(NS * 128, D)
    for k in range(4):
        block = ((place[0] + k) % 4) * 2 + place[1]
        out[k] = mm(onehot_rows(ids, block * 256, 256), rows).astype(out.dtype)


def call(kernel, outs, specs, args, flops, scratch=(), out_specs=None, vmem=26 * MB):
    return pl.pallas_call(
        kernel,
        out_shape=[jax.ShapeDtypeStruct(*o) for o in outs],
        in_specs=specs,
        out_specs=out_specs or [VM] * len(outs),
        scratch_shapes=list(scratch),
        compiler_params=pltpu.CompilerParams(vmem_limit_bytes=vmem),
        cost_estimate=pl.CostEstimate(
            flops=flops, bytes_accessed=4 * MB, transcendentals=0
        ),
    )(*args)


def per_device(
    table, hist_bias, hist_shard, hist_row, lengths, panel_row, req_user, req_cand, d_out
):
    def swap(a):
        return lax.all_to_all(a, "dev", split_axis=0, concat_axis=0, tiled=True)

    slot, first = call(
        prepare_kernel,
        [((1, H), I32), ((NS, ASK, D), BF)],
        [VM, VM, SM, VM],
        (hist_shard.reshape(1, H), hist_row.reshape(1, H), panel_row, table),
        10**9,
    )
    asked, panel, fetched = call(
        fetch_kernel,
        [((NS, 128), I32), ((PG, D), BF), ((NS, CAP, D), BF)],
        [VM, VM],
        (swap(first), table),
        4 * 10**9,
        out_specs=[VM, VM, HB],
        scratch=[pltpu.VMEM((NS, CAP, D), BF), pltpu.SemaphoreType.DMA((4,))],
    )
    got = swap(fetched)
    q, q_t, up_t, slot_col, bias_col, pos_col, cand_row, starts = call(
        requests_kernel,
        [
            ((H, D), BF),
            ((D, H), BF),
            ((D, H), BF),
            ((H, 128), I32),
            ((H, 128), F32),
            ((H, 128), I32),
            ((1, H), I32),
            ((4,), I32),
        ],
        [VM] * 6,
        (
            req_user.reshape(1, H),
            req_cand.reshape(1, H),
            hist_bias.reshape(1, H),
            slot,
            d_out,
            panel,
        ),
        8 * 10**9,
        out_specs=[VM] * 7 + [SM],
    )
    bias_grad, att_t, send = call(
        attend_kernel,
        [((1, H), F32), ((D, H), BF), ((NS, 128, D), BF)],
        [VM] * 3 + [SM] * 2 + [HB] * 5,
        (
            got.reshape(NS * CAP, D),
            slot,
            cand_row,
            lengths.reshape(4),
            starts,
            slot_col,
            bias_col,
            q,
            q_t,
            up_t,
        ),
        20 * 10**9,
        out_specs=[VM, HB, HB],
        scratch=[
            pltpu.VMEM((H, 128), I32),
            pltpu.VMEM((H, 128), F32),
            pltpu.VMEM((H, D), BF),
            pltpu.VMEM((D, H), BF),
            pltpu.VMEM((D, H), BF),
            pltpu.VMEM((D, H), BF),
            pltpu.VMEM((NS, 128, D), BF),
            pltpu.VMEM((H, D), BF),
            pltpu.VMEM((D, H), BF),
            pltpu.VMEM((H, 128), I32),
            pltpu.VMEM((H, D), F32),
            pltpu.VMEM((H, 128), F32),
            pltpu.VMEM((D, H), BF),
            pltpu.SemaphoreType.DMA((10,)),
        ],
        vmem=59 * MB,
    )
    arrived = swap(send)
    [attended] = call(
        restore_kernel, [((H, D), BF)], [VM, VM], (pos_col, att_t), 3 * 10**9
    )
    asked, attended = lax.optimization_barrier((asked, attended))
    grp = lax.axis_index("grp")
    y, core = grp // 2, grp % 2
    specs = [SM, SM, VM, VM]
    [theirs] = call(
        gradient_kernel,
        [((4, 256, D), BF)],
        specs,
        (jnp.stack([y, 1 - core]), panel_row, asked, arrived),
        3 * 10**9,
    )
    n_grp = lax.axis_size("grp")
    theirs = lax.ppermute(theirs, "grp", [(i, i ^ 1) for i in range(n_grp)])
    [mine] = call(
        gradient_kernel,
        [((4, 256, D), F32)],
        specs,
        (jnp.stack([y, core]), panel_row, asked, arrived),
        3 * 10**9,
    )
    pair = mine + theirs.astype(F32)
    total = pair[0]
    for k in (1, 2, 3):
        hop = [(i, (i // 2 + k) % 4 * 2 + i % 2) for i in range(n_grp)]
        total = total + lax.ppermute(pair[k].astype(BF), "grp", hop).astype(F32)
    return (attended, total[None], bias_grad.reshape(H))


def solution(mesh):
    return jax.shard_map(
        per_device,
        mesh=mesh,
        in_specs=(
            P("dev", None),
            P(("grp", "dev")),
            P(("grp", "dev"), None),
            P(("grp", "dev")),
            P(("grp", "dev"), None),
            P(("grp", "dev")),
            P(("grp", "dev")),
            P(("grp", "dev")),
            P(("grp", "dev"), None),
        ),
        out_specs=(P(("grp", "dev"), None), P("dev", "grp", None), P(("grp", "dev"))),
        check_vma=False,
    )
```

```python
import functools

import jax
import jax.numpy as jnp
from jax import lax
from jax.experimental import pallas as pl
from jax.experimental.pallas import tpu as pltpu
from jax.sharding import PartitionSpec as P

BF = jnp.bfloat16
F32 = jnp.float32
I32 = jnp.int32
H = 2048
D = 256
NS = 32
CAP = 96
CP = 32
ASK = 40
PG = NS * CP
TILE = 256
GROUP = 1
WIDTHS = (256, 512, 768, 1024, 1280, 1536, 2048)
MB = 1 << 20

VM = pl.BlockSpec(memory_space=pltpu.VMEM)
SM = pl.BlockSpec(memory_space=pltpu.SMEM)
HB = pl.BlockSpec(memory_space=pltpu.HBM)


def iota(shape, dim):
    return lax.broadcasted_iota(I32, shape, dim)


def mm(a, b):
    return jnp.dot(a, b, preferred_element_type=F32)


def mm_nt(a, b):
    return lax.dot_general(a, b, (((1,), (1,)), ((), ())), preferred_element_type=F32)


def ones_where(mask):
    return jnp.where(mask, 1.0, 0.0).astype(BF)


def onehot_lanes(column, count):
    lane = iota(column.shape, 1).astype(column.dtype)
    return jnp.concatenate(
        [ones_where(column == lane + 128 * t) for t in range(count // 128)], axis=1
    )


def onehot_rows(row, base, count):
    return ones_where(iota((count, row.shape[1]), 0) + base == row)


def as_column(row):
    return jnp.transpose(jnp.broadcast_to(row.astype(F32), (128, row.shape[1])))


def ranks(member):
    width = 256
    upper = ones_where(iota((width, width), 0) < iota((width, width), 1))
    ahead, carry = [], jnp.zeros((member.shape[0], 1), F32)
    for b in range(member.shape[1] // width):
        part = member[:, b * width : (b + 1) * width]
        ahead.append(mm(part.astype(BF), upper) + carry)
        carry = carry + jnp.sum(part, axis=1, keepdims=True)
    return jnp.sum(jnp.concatenate(ahead, axis=1) * member, axis=0, keepdims=True)


def prepare_kernel(shard, row, panel_row, table_hbm, slot, out, table, sem):
    load = pltpu.make_async_copy(table_hbm, table, sem)
    load.start()
    target = shard[...]
    member = jnp.where(iota((NS, H), 0) == target, 1.0, 0.0)
    rank = ranks(member).astype(I32)
    slot[...] = target * CAP + rank
    here = iota((128, H), 0) == rank
    low = jnp.where(here, (row[...] & 127).astype(F32), 0.0).astype(BF)
    high = jnp.where(here, (row[...] >> 7).astype(F32), 0.0).astype(BF)
    ids = mm_nt(member.astype(BF), jnp.concatenate([low, high], axis=0))
    own = jnp.zeros((CP, 128), I32)
    for c in range(CP):
        own = jnp.where(iota((CP, 128), 0) == c, panel_row[c], own)
    load.wait()
    rows = mm(onehot_lanes(own, H), table[...])
    pad = jnp.zeros((ASK - CP - 1, D), F32)
    for s in range(NS):
        out[s] = jnp.concatenate([rows, ids[s : s + 1, :], pad], axis=0).astype(BF)


def fetch_kernel(first, table, asked, panel, out, rows, sems):
    both = [first[s].astype(F32)[CP : CP + 1, :] for s in range(NS)]
    both = jnp.concatenate(both, axis=0)
    ids = both[:, :128] + 128.0 * both[:, 128:]
    asked[...] = ids.astype(I32)
    ids = jnp.transpose(jnp.concatenate([ids, jnp.zeros((96, 128), F32)], axis=0))
    copies = []
    for n in range(4):
        part = pl.ds(n * 8, 8)
        hot = jnp.concatenate(
            [
                onehot_lanes(jnp.broadcast_to(ids[:CAP, s : s + 1], (CAP, 128)), H)
                for s in range(n * 8, n * 8 + 8)
            ],
            axis=0,
        )
        rows[part] = mm(hot, table[...]).astype(BF).reshape(8, CAP, D)
        copies.append(pltpu.make_async_copy(rows.at[part], out.at[part], sems.at[n]))
        copies[-1].start()
    for s in range(NS):
        panel[s * CP : s * CP + CP, :] = first[s, :CP, :]
    for copy in copies:
        copy.wait()


def requests_kernel(
    user, cand, bias, slot, d_out, panel, q, q_t, up_t, slot_col, bias_col, pos_col, cand_row, starts
):
    own = user[...]
    member = jnp.where(iota((8, H), 0) == own, 1.0, 0.0)
    pos = ranks(member)
    begin = [jnp.sum(jnp.where(own < u, 1.0, 0.0)).astype(I32) for u in (1, 2, 3)]
    starts[0] = 0
    for u in (1, 2, 3):
        starts[u] = begin[u - 1]
        pos = pos + jnp.where(own == u, begin[u - 1].astype(F32), 0.0)
    pos = pos.astype(I32)
    slot_col[...] = as_column(slot[...]).astype(I32)
    bias_col[...] = as_column(bias[...])
    pos_col[...] = as_column(pos).astype(I32)
    low = as_column(cand[...] & 127).astype(BF)
    high = as_column(cand[...] >> 7).astype(BF)
    right = jnp.concatenate([d_out[...], low, high], axis=1)
    for i in range(4):
        part = slice(i * 512, (i + 1) * 512)
        got = mm(onehot_rows(pos, i * 512, 512), right)
        up_t[:, part] = jnp.transpose(got[:, :D]).astype(BF)
        which = got[:, D : D + 128] + 128.0 * got[:, D + 128 :]
        cand_row[:, part] = jnp.transpose(which)[:1, :].astype(I32)
        query = mm(onehot_lanes(which, PG), panel[...]) * (D**-0.5)
        q[part, :] = query.astype(BF)
        q_t[:, part] = jnp.transpose(query).astype(BF)


def attend_kernel(
    got_hbm, slot, cand_row, lengths, starts, slot_hbm, bias_hbm, q_hbm, q_t_hbm, up_t_hbm,
    bias_grad, att_hbm, send_hbm,
    got, slot_col, bias_col, q, q_t, up_t, att_t, send,
    key, key_t, seg, d_key, d_bias, dq_t, sems,
):
    loads = [
        pltpu.make_async_copy(a, b, sems.at[n])
        for n, (a, b) in enumerate(
            [
                (got_hbm, got),
                (slot_hbm, slot_col),
                (bias_hbm, bias_col),
                (q_t_hbm, q_t),
                (up_t_hbm, up_t),
                (q_hbm, q),
            ]
        )
    ]
    for load in loads:
        load.start()
    d_key[...] = jnp.zeros_like(d_key)
    d_bias[...] = jnp.zeros_like(d_bias)
    loads[0].wait()
    loads[1].wait()
    def gather(i, carry):
        part = pl.ds(pl.multiple_of(i * 512, 512), 512)
        rows = mm(onehot_lanes(slot_col[part, :], NS * CAP), got[...])
        key[part, :] = rows.astype(BF)
        key_t[:, part] = jnp.transpose(rows).astype(BF)
        return carry

    lax.fori_loop(0, 4, gather, 0)
    ends = [lengths[0]]
    for u in (1, 2, 3):
        ends.append(ends[-1] + lengths[u])
    place = iota((H, 128), 0)
    seg[...] = sum((place >= ends[u]).astype(I32) for u in range(3))
    for load in loads[2:]:
        load.wait()

    def owner_of(r):
        return sum((r >= starts[u]).astype(I32) for u in (1, 2, 3))

    def step(tiles, width, firsts):
        cols = [pl.ds(pl.multiple_of(i * TILE, TILE), TILE) for i in tiles]
        wins = [pl.ds(pl.multiple_of(f, 128), width) for f in firsts]
        each = range(len(tiles))

        def wide(a):
            return jnp.concatenate([a] * (TILE // 128), axis=1)

        k = [key[w, :] for w in wins]
        score = [mm(k[n], q_t[:, cols[n]]) + wide(bias_col[wins[n], :]) for n in each]
        weight, weight_b = [], []
        for n in each:
            owner = owner_of(iota((1, TILE), 1) + tiles[n] * TILE)
            s = jnp.where(wide(seg[wins[n], :]) == owner, score[n], -1e30)
            raised = jnp.exp(s - jnp.max(s, axis=0, keepdims=True))
            weight.append(raised * (1.0 / jnp.sum(raised, axis=0, keepdims=True)))
            weight_b.append(weight[n].astype(BF))
        mixed = [mm(key_t[:, wins[n]], weight_b[n]) for n in each]
        rounded, total = [], []
        for n in each:
            m = mixed[n]
            inverse = lax.rsqrt(jnp.mean(m * m, axis=0, keepdims=True) + 1e-6)
            att_t[:, cols[n]] = (m * inverse).astype(BF)
            up = up_t[:, cols[n]].astype(F32)
            along = jnp.mean(up * m, axis=0, keepdims=True)
            d_mixed = inverse * up - m * (inverse * inverse * inverse * along)
            rounded.append(d_mixed.astype(BF))
            total.append(jnp.sum(rounded[n].astype(F32) * m, axis=0, keepdims=True))
        d_weight = [mm(k[n], rounded[n]) for n in each]
        d_score_b = []
        for n in each:
            d_score = weight[n] * (d_weight[n] - total[n])
            d_score_b.append(d_score.astype(BF))
            d_bias[wins[n], :] += sum(
                d_score[:, c : c + 128] for c in range(0, TILE, 128)
            )
        for n in each:
            d_mixed = jnp.transpose(rounded[n].astype(F32)).astype(BF)
            left = jnp.concatenate([weight_b[n], d_score_b[n]], axis=1)
            right = jnp.concatenate([d_mixed, q[cols[n], :]], axis=0)
            d_key[wins[n], :] += mm(left, right)
            dq_t[:, cols[n]] = (mm(key_t[:, wins[n]], d_score_b[n]) * (D**-0.5)).astype(BF)

    def window(i):
        u_first = owner_of(i * TILE)
        u_last = owner_of(i * TILE + TILE - 1)
        low, high = jnp.int32(0), ends[0]
        for u in (1, 2, 3):
            low = jnp.where(u_first >= u, ends[u - 1], low)
            high = jnp.where(u_last >= u, ends[u], high)
        first = (low // 128) * 128
        return first, high - first

    def together(i, carry):
        tiles = [i * GROUP + n for n in range(GROUP)]
        found = [window(t) for t in tiles]
        need = functools.reduce(jnp.maximum, [f[1] for f in found])
        for n, width in enumerate(WIDTHS):
            fits = need <= width
            if n > 0:
                fits = fits & (need > WIDTHS[n - 1])

            @pl.when(fits)
            def _():
                step(tiles, width, [jnp.minimum(f[0], H - width) for f in found])

        return carry

    lax.fori_loop(0, H // (TILE * GROUP), together, 0)
    stores = [pltpu.make_async_copy(att_t, att_hbm, sems.at[6])]
    stores[0].start()
    term = d_key[...].astype(BF)

    def scatter(n, carry):
        part = pl.ds(n * 8, 8)
        out = mm(onehot_rows(slot[...], n * 8 * CAP, 8 * CAP), term).astype(BF)
        send[part, :CAP, :] = out.reshape(8, CAP, D)
        out = mm_nt(onehot_rows(cand_row[...], n * 8 * CP, 8 * CP), dq_t[...]).astype(BF)
        send[part, CAP:, :] = out.reshape(8, CP, D)
        pltpu.make_async_copy(send.at[part], send_hbm.at[part], sems.at[7 + n]).start()
        return carry

    lax.fori_loop(0, 4, scatter, 0)
    for n in range(4):
        part = pl.ds(n * 8, 8)
        stores.append(
            pltpu.make_async_copy(send.at[part], send_hbm.at[part], sems.at[7 + n])
        )
    bias_grad[...] = jnp.sum(jnp.transpose(d_bias[...]), axis=0, keepdims=True)
    for store in stores:
        store.wait()


def restore_kernel(pos_col, att_t, out):
    for i in range(4):
        part = slice(i * 512, (i + 1) * 512)
        out[part, :] = mm_nt(onehot_lanes(pos_col[part, :], H), att_t[...]).astype(BF)


def gradient_kernel(place, panel_row, asked, arrived, out):
    ids = asked[...]
    lane = iota((1, 128), 1)
    own = jnp.zeros((1, 128), I32)
    for c in range(CP):
        own = jnp.where(lane == CAP + c, panel_row[c], own)
    ids = jnp.concatenate(
        [jnp.where(lane >= CAP, own, ids[s : s + 1, :]) for s in range(NS)], axis=1
    )
    rows = arrived[...].reshape(NS * 128, D)
    for k in range(4):
        block = ((place[0] + k) % 4) * 2 + place[1]
        out[k] = mm(onehot_rows(ids, block * 256, 256), rows).astype(out.dtype)


def call(kernel, outs, specs, args, flops, scratch=(), out_specs=None, vmem=26 * MB):
    return pl.pallas_call(
        kernel,
        out_shape=[jax.ShapeDtypeStruct(*o) for o in outs],
        in_specs=specs,
        out_specs=out_specs or [VM] * len(outs),
        scratch_shapes=list(scratch),
        compiler_params=pltpu.CompilerParams(vmem_limit_bytes=vmem),
        cost_estimate=pl.CostEstimate(
            flops=flops, bytes_accessed=4 * MB, transcendentals=0
        ),
    )(*args)


def attend(*operands):
    return call(
        attend_kernel,
        [((1, H), F32), ((D, H), BF), ((NS, 128, D), BF)],
        [HB] + [VM] * 2 + [SM] * 2 + [HB] * 5,
        operands,
        20 * 10**9,
        out_specs=[VM, HB, HB],
        scratch=[
            pltpu.VMEM((NS * CAP, D), BF),
            pltpu.VMEM((H, 128), I32),
            pltpu.VMEM((H, 128), F32),
            pltpu.VMEM((H, D), BF),
            pltpu.VMEM((D, H), BF),
            pltpu.VMEM((D, H), BF),
            pltpu.VMEM((D, H), BF),
            pltpu.VMEM((NS, 128, D), BF),
            pltpu.VMEM((H, D), BF),
            pltpu.VMEM((D, H), BF),
            pltpu.VMEM((H, 128), I32),
            pltpu.VMEM((H, D), F32),
            pltpu.VMEM((H, 128), F32),
            pltpu.VMEM((D, H), BF),
            pltpu.SemaphoreType.DMA((11,)),
        ],
        vmem=59 * MB,
    )


def per_device(
    table, hist_bias, hist_shard, hist_row, lengths, panel_row, req_user, req_cand, d_out
):
    def swap(a):
        return lax.all_to_all(a, "dev", split_axis=0, concat_axis=0, tiled=True)

    slot, first = call(
        prepare_kernel,
        [((1, H), I32), ((NS, ASK, D), BF)],
        [VM, VM, SM, HB],
        (hist_shard.reshape(1, H), hist_row.reshape(1, H), panel_row, table),
        10**9,
        scratch=[pltpu.VMEM((H, D), BF), pltpu.SemaphoreType.DMA],
        vmem=59 * MB,
    )
    asked, panel, fetched = call(
        fetch_kernel,
        [((NS, 128), I32), ((PG, D), BF), ((NS, CAP, D), BF)],
        [VM, VM],
        (swap(first), table),
        4 * 10**9,
        out_specs=[VM, VM, HB],
        scratch=[
            pltpu.VMEM((NS, CAP, D), BF),
            pltpu.SemaphoreType.DMA((4,)),
        ],
    )
    got = swap(fetched)
    q, q_t, up_t, slot_col, bias_col, pos_col, cand_row, starts = call(
        requests_kernel,
        [
            ((H, D), BF),
            ((D, H), BF),
            ((D, H), BF),
            ((H, 128), I32),
            ((H, 128), F32),
            ((H, 128), I32),
            ((1, H), I32),
            ((4,), I32),
        ],
        [VM] * 6,
        (
            req_user.reshape(1, H),
            req_cand.reshape(1, H),
            hist_bias.reshape(1, H),
            slot,
            d_out,
            panel,
        ),
        8 * 10**9,
        out_specs=[VM] * 7 + [SM],
    )
    bias_grad, att_t, send = attend(
        got.reshape(NS * CAP, D),
        slot,
        cand_row,
        lengths.reshape(4),
        starts,
        slot_col,
        bias_col,
        q,
        q_t,
        up_t,
    )
    arrived = swap(send)
    [attended] = call(
        restore_kernel, [((H, D), BF)], [VM, VM], (pos_col, att_t), 3 * 10**9
    )
    asked, attended = lax.optimization_barrier((asked, attended))
    grp = lax.axis_index("grp")
    y, core = grp // 2, grp % 2
    specs = [SM, SM, VM, VM]
    [theirs] = call(
        gradient_kernel,
        [((4, 256, D), BF)],
        specs,
        (jnp.stack([y, 1 - core]), panel_row, asked, arrived),
        3 * 10**9,
    )
    n_grp = lax.axis_size("grp")
    theirs = lax.ppermute(theirs, "grp", [(i, i ^ 1) for i in range(n_grp)])
    [mine] = call(
        gradient_kernel,
        [((4, 256, D), F32)],
        specs,
        (jnp.stack([y, core]), panel_row, asked, arrived),
        3 * 10**9,
    )
    pair = mine + theirs.astype(F32)
    total = pair[0]
    for k in (1, 2, 3):
        hop = [(i, (i // 2 + k) % 4 * 2 + i % 2) for i in range(n_grp)]
        total = total + lax.ppermute(pair[k].astype(BF), "grp", hop).astype(F32)
    return (attended, total[None], bias_grad.reshape(H))


def solution(mesh):
    return jax.shard_map(
        per_device,
        mesh=mesh,
        in_specs=(
            P("dev", None),
            P(("grp", "dev")),
            P(("grp", "dev"), None),
            P(("grp", "dev")),
            P(("grp", "dev"), None),
            P(("grp", "dev")),
            P(("grp", "dev")),
            P(("grp", "dev")),
            P(("grp", "dev"), None),
        ),
        out_specs=(P(("grp", "dev"), None), P("dev", "grp", None), P(("grp", "dev"))),
        check_vma=False,
    )
```
